1024 devices in a mesh: row: 8 (over y), col: 128 (over z, x, core).
Axes of the slice: x: 8, y: 8, z: 8, core: 2. Of those that a mesh axis runs over, the one named last changes fastest.
Arguments:
- pivot: float32 [1024, 1024], replicated, may hold values from -1 to 2
- col_panel: float32 [4096, 1024], P('row', 'col'), may hold values from -0.25 to 0.25
- row_panel: float32 [1024, 32768], P('row', 'col'), may hold values from -6 to 6
- trailing: float32 [4096, 32768], P('row', 'col'), may hold values from -6 to 6
Outputs:
- updated: float32 [4096, 32768], P('row', 'col')
The draws below stay inside these ranges and needn't reach their ends.
All inputs are finite; a program needn't handle non-finite values.
Results may differ from the reference program's by a relative error of at most 0.000061.
Values sent between devices are 32-bit elements; how exact they have to be, the bound alone decides.
A program may use at most 64 MiB of HBM per device.

```python
import math
import jax
import jax.numpy as jnp
from jax import lax

B = 512
TRAIL_ROWS = 4096
TRAIL_COLS = 32768


def draw_pivot(key, part):
    noise = jax.random.normal(key, (2 * B, 2 * B), jnp.float32)
    return jnp.eye(2 * B, dtype=jnp.float32) + 0.25 / math.sqrt(B) * noise


def block_scale(own_key, extent, pieces, smallest, high):
    loudness, own = 1.0, jax.random.fold_in(own_key, 6)
    for dim, parts in pieces:
        heights = jnp.exp(jax.random.uniform(jax.random.fold_in(own, dim), (parts,), jnp.float32, smallest / len(pieces), high / len(pieces)))
        loudness = loudness * jnp.repeat(heights, extent[dim] // parts).reshape([-1 if axis == dim else 1 for axis in range(len(extent))])
    return loudness


def gaussian(rng, extent, deviation, bound, pieces=(), held_as=jnp.bfloat16):
    array = deviation * jax.random.normal(rng, extent, jnp.float32)
    if pieces:
        array = array * block_scale(rng, extent, pieces, -0.22, 0.18)
    return jnp.clip(array, -bound, bound).astype(held_as)


def setup_inputs(seed: int = 0) -> dict:
    keys = jax.random.split(jax.random.key(seed), 5)
    return {
        "pivot": draw_pivot(jax.random.fold_in(keys[4], 71), 0),
        "col_panel": gaussian(keys[1], (TRAIL_ROWS, 2 * B), B ** -0.5, 0.25, ((0, 8), (1, 128)), jnp.float32),
        "row_panel": gaussian(keys[2], (2 * B, TRAIL_COLS), 1.0, 6.0, ((0, 8), (1, 128)), jnp.float32),
        "trailing": gaussian(keys[3], (TRAIL_ROWS, TRAIL_COLS), 1.0, 6.0, ((0, 8), (1, 128)), jnp.float32),
    }


def product(left, right):
    return jnp.dot(left, right, precision=lax.Precision.HIGHEST, preferred_element_type=jnp.float32)


def newton_inverse(matrix):
    identity = jnp.eye(matrix.shape[0], dtype=jnp.float32)
    initial = 2.0 * identity - matrix
    return product(initial, 2.0 * identity - product(matrix, initial))


def reference(pivot, col_panel, row_panel, trailing):
    top_left = pivot[:B, :B]
    top_right = pivot[:B, B:]
    low_left = pivot[B:, :B]
    low_right = pivot[B:, B:]
    inverse_one = newton_inverse(top_left)
    multiplier = product(low_left, inverse_one)
    schur = low_right - product(multiplier, top_right)
    inverse_two = newton_inverse(schur)
    factor_one = product(col_panel[:, :B], inverse_one)
    factor_two = product(col_panel[:, B:] - product(factor_one, top_right), inverse_two)
    first_rows = row_panel[:B]
    rows_two = row_panel[B:] - product(multiplier, first_rows)
    return trailing - product(factor_one, first_rows) - product(factor_two, rows_two)
```

```python
import jax
import jax.numpy as jnp
from jax import lax
from jax.experimental import pallas as pl
from jax.experimental.pallas import tpu as pltpu
from jax.sharding import PartitionSpec as P

B = 512
N = 8
MESH = pl.DeviceIdType.MESH
F32 = jnp.float32
BF16 = jnp.bfloat16
GROUPS = ((0, 4), (4, 2), (6, 1), (7, 1))


def split(value):
    high = value.astype(BF16)
    return high, (value - high.astype(F32)).astype(BF16)


def dot(left, right):
    return jnp.dot(left, right, preferred_element_type=F32)


def product(left, right):
    return dot(left[0], right[0]) + (dot(left[0], right[1]) + dot(left[1], right[0]))


def kernel(pivot_ref, col_ref, row_ref, trail_ref, out_ref, piv, rb, cb, trail, f_a, f_b, h_a, h_b, h_inv1, h_n, h_ll, h_inv2, h_y,
           loc, zs, zr, xs, xr, bs, br, rs, rr, inz, inx, iny, ins):
    y = lax.axis_index("row")
    col = lax.axis_index("col")
    c = lax.rem(col, 2)
    x = lax.rem(col // 2, N)
    z = col // (2 * N)

    def column(z_, x_, c_):
        return (z_ * N + x_) * 2 + c_

    def first(y_, z_, x_, c_):
        return jnp.where((y_ == 0) & (z_ == 0) & (x_ == 0) & (c_ == 0), 100, 0)

    def ringed(v):
        return 2 * jnp.minimum(v, N - v) - jnp.where(v < N // 2, 1, 0)

    mine = first(y, z, x, c)
    partners = []
    zp, xp, yp = [], [], []
    for k in range(N):
        zp.append((y, column(k, x, c)))
        partners.append((zp[k], z != k, k + first(y, k, x, c) > z + mine, inz.at[z], inz.at[k]))
    for k in range(N):
        xp.append((y, column(z, k, c)))
        partners.append((xp[k], x != k, ringed(jnp.int32(k)) + first(y, z, k, c) > ringed(x) + mine, inx.at[x], inx.at[k]))
    for k, off in enumerate((1, N - 1, 2, N - 2)):
        other = lax.rem(y + off, N)
        yp.append((other, col))
        partners.append((yp[k], None, ringed(other) + first(other, z, x, c) > ringed(y) + mine, iny.at[k ^ 1], iny.at[k]))
    sib = (y, column(z, x, 1 - c))
    partners.append((sib, None, (c == 1), ins.at[0], ins.at[0]))

    def both(a, b):
        return b if a is None else a & b

    local = []
    for k, (r, q) in enumerate(((0, 0), (0, 1), (1, 0), (1, 1))):
        part = (pl.ds(r * B, B), pl.ds(q * B, B))
        local.append(pltpu.make_async_copy(pivot_ref.at[part], piv.at[part], loc.at[k]))
    own_c = pltpu.make_async_copy(col_ref, cb.at[z, x, c], loc.at[4])
    own_r = pltpu.make_async_copy(row_ref, rb.at[y], loc.at[5])
    own_t = pltpu.make_async_copy(trail_ref, trail, loc.at[6])
    own_c.start()
    local[0].start()

    barrier = pltpu.get_barrier_semaphore()
    count = jnp.int32(0)
    for dev, there, later, _, _ in partners:
        earlier = both(there, jnp.logical_not(later))
        count = count + earlier.astype(jnp.int32)

        @pl.when(both(there, later))
        def _():
            pl.semaphore_signal(barrier, inc=1, device_id=dev, device_id_type=MESH)

    @pl.when(count > 0)
    def _():
        pl.semaphore_wait(barrier, count)

    def remote(src, dst, send, recv, dev):
        return pltpu.make_async_remote_copy(src_ref=src, dst_ref=dst, send_sem=send, recv_sem=recv, device_id=dev, device_id_type=MESH)

    def z_copy(k, src_z=None):
        return remote(col_ref, cb.at[z, x, c], zs.at[k], zr.at[z], zp[k])

    def z_wait(k):
        remote(col_ref, cb.at[k, x, c], zs.at[k], zr.at[k], zp[k]).wait_recv()

    for k in range(N):
        _, there, later, _, _ = partners[k]

        @pl.when(there & jnp.logical_not(later))
        def _():
            z_copy(k).start()

    for dev, there, later, theirs, _ in partners:
        @pl.when(both(there, jnp.logical_not(later)))
        def _():
            pl.semaphore_signal(theirs, inc=1, device_id=dev, device_id_type=MESH)

    def admit(i):
        _, there, later, _, own = partners[i]

        @pl.when(both(there, later))
        def _():
            pl.semaphore_wait(own, 1)

    for k in range(1, 4):
        local[k].start()
    own_r.start()
    own_t.start()

    half = B // 8

    def r_copy(k):
        src_y = lax.rem(y + (0, 0, 0, 0, N - 2, 2, N - 2, 2)[k], N)
        dev = yp[(0, 1, 2, 3, 0, 1, 2, 3)[k]]
        if k < 4:
            src, dst = row_ref, rb.at[y]
        elif k < 6:
            src = dst = rb.at[src_y]
        else:
            src = dst = rb.at[src_y, pl.ds((k - 6) * half, half)]
        return remote(src, dst, rs.at[k], rr.at[k], dev)

    def r_wait(k):
        at = lax.rem(y + (N - 1, 1, N - 2, 2, N - 3, 3, N - 4, 4)[k], N)
        ref = rb.at[at] if k < 6 else rb.at[at, pl.ds((k - 6) * half, half)]
        remote(ref, ref, rs.at[k], rr.at[k], yp[0]).wait_recv()

    for k in (2, 3, 0, 1):
        admit(2 * N + k)
        r_copy(k).start()
    admit(2 * N + 4)

    eye = (lax.broadcasted_iota(jnp.int32, (B, B), 0) == lax.broadcasted_iota(jnp.int32, (B, B), 1)).astype(F32)

    def load(ref):
        return ref[0], ref[1]

    def store(ref, value):
        ref[0], ref[1] = split(value)

    local[0].wait()
    e = eye - piv[:B, :B]
    f_a[...] = e
    store(h_a, e)
    square = product(load(h_a), load(h_a))
    f_b[...] = square
    store(h_b, square)
    store(h_inv1, eye + f_a[...] + f_b[...] + product(load(h_a), load(h_b)))
    local[1].wait()
    store(h_n, product(load(h_inv1), split(piv[:B, B:])))
    local[2].wait()
    local[3].wait()
    store(h_ll, piv[B:, :B])
    e = eye - piv[B:, B:] + product(load(h_ll), load(h_n))
    f_a[...] = e
    store(h_a, e)
    r_wait(2)
    r_copy(4).start()
    r_copy(6).start()
    r_wait(3)
    r_copy(5).start()
    r_copy(7).start()
    square = product(load(h_a), load(h_a))
    f_b[...] = square
    store(h_b, square)
    store(h_inv2, eye + f_a[...] + f_b[...] + product(load(h_a), load(h_b)))

    own_c.wait()
    for k in range(N):
        admit(N + k)

    def x_copy(g, k):
        z0, n = GROUPS[g]
        ref = cb.at[pl.ds(z0, n), x, c]
        return remote(ref, ref, xs.at[g, k], xr.at[g, x], xp[k])

    def x_wait(g, k):
        z0, n = GROUPS[g]
        ref = cb.at[pl.ds(z0, n), k, c]
        remote(ref, ref, xs.at[g, k], xr.at[g, k], xp[k]).wait_recv()

    for g, (z0, n) in enumerate(GROUPS):
        for k in range(z0, z0 + n):
            _, there, later, _, own = partners[k]

            @pl.when(there & later)
            def _():
                pl.semaphore_wait(own, 1)
                z_copy(k).start()

            @pl.when(there)
            def _():
                z_wait(k)

        for k in range(N):
            @pl.when(x != k)
            def _():
                x_copy(g, k).start()

    def b_copy(g):
        z0, n = GROUPS[g]
        ref = cb.at[pl.ds(z0, n), :, c]
        return remote(ref, ref, bs.at[g], br.at[g], sib)

    def b_wait(g):
        z0, n = GROUPS[g]
        ref = cb.at[pl.ds(z0, n), :, 1 - c]
        remote(ref, ref, bs.at[g], br.at[g], sib).wait_recv()

    def share(g):
        for k in range(N):
            @pl.when(x != k)
            def _():
                x_wait(g, k)
        b_copy(g).start()

    share(0)
    own_r.wait()
    for k in (0, 1, 4, 5, 6, 7):
        r_wait(k)
    first_rows = rb[0:4].reshape(B, 2 * 128)
    second_rows = rb[4:8].reshape(B, 2 * 128)
    u = product(load(h_inv1), split(first_rows))
    rest = second_rows - product(load(h_ll), split(u))
    share(1)
    y_two = split(product(load(h_inv2), split(rest)))
    h_y[0, B:], h_y[1, B:] = y_two
    h_y[0, :B], h_y[1, :B] = split(u - product(load(h_n), y_two))
    own_t.wait()

    def eliminate(g):
        z0, n = GROUPS[g]
        k0, kn = z0 * 128, n * 128
        b_wait(g)
        left = cb[z0:z0 + n].reshape(kn, B).T
        return product(split(left), (h_y[0, k0:k0 + kn], h_y[1, k0:k0 + kn]))

    trail[...] = trail[...] - eliminate(0)
    share(2)
    trail[...] = trail[...] - eliminate(1)
    share(3)
    trail[...] = trail[...] - eliminate(2)
    out_ref[...] = trail[...] - eliminate(3)

    for k in range(N):
        @pl.when(z != k)
        def _():
            z_copy(k).wait_send()

        @pl.when(x != k)
        def _():
            for g in range(len(GROUPS)):
                x_copy(g, k).wait_send()

    for k in range(8):
        r_copy(k).wait_send()
    for g in range(len(GROUPS)):
        b_copy(g).wait_send()


def local_step(pivot, col_panel, row_panel, trailing):
    pair = pltpu.VMEM((2, B, B), BF16)
    return pl.pallas_call(
        kernel,
        out_shape=jax.ShapeDtypeStruct(trailing.shape, F32),
        in_specs=[pl.BlockSpec(memory_space=pl.ANY)] * 4,
        out_specs=pl.BlockSpec(memory_space=pltpu.VMEM),
        scratch_shapes=[
            pltpu.VMEM((2 * B, 2 * B), F32),
            pltpu.VMEM((N, 128, 256), F32),
            pltpu.VMEM((N, N, 2, 8, B), F32),
            pltpu.VMEM((B, 256), F32),
            pltpu.VMEM((B, B), F32),
            pltpu.VMEM((B, B), F32),
            pair, pair, pair, pair, pair, pair,
            pltpu.VMEM((2, 2 * B, 256), BF16),
            pltpu.SemaphoreType.DMA((7,)),
            pltpu.SemaphoreType.DMA((N,)),
            pltpu.SemaphoreType.DMA((N,)),
            pltpu.SemaphoreType.DMA((len(GROUPS), N)),
            pltpu.SemaphoreType.DMA((len(GROUPS), N)),
            pltpu.SemaphoreType.DMA((len(GROUPS),)),
            pltpu.SemaphoreType.DMA((len(GROUPS),)),
            pltpu.SemaphoreType.DMA((8,)),
            pltpu.SemaphoreType.DMA((8,)),
            pltpu.SemaphoreType.REGULAR((N,)),
            pltpu.SemaphoreType.REGULAR((N,)),
            pltpu.SemaphoreType.REGULAR((4,)),
            pltpu.SemaphoreType.REGULAR((1,)),
        ],
        compiler_params=pltpu.CompilerParams(collective_id=0, has_side_effects=True, vmem_limit_bytes=56 << 20),
        name="eliminate",
    )(pivot, col_panel.T, row_panel, trailing)


def solution(mesh):
    return jax.shard_map(
        local_step,
        mesh=mesh,
        in_specs=(P(), P("row", "col"), P("row", "col"), P("row", "col")),
        out_specs=P("row", "col"),
        check_vma=False,
    )
```

```python
import jax
import jax.numpy as jnp
from jax import lax
from jax.experimental import pallas as pl
from jax.experimental.pallas import tpu as pltpu
from jax.sharding import PartitionSpec as P

B = 512
N = 8
MESH = pl.DeviceIdType.MESH
F32 = jnp.float32
BF16 = jnp.bfloat16
GROUPS = ((0, 2), (2, 2), (4, 1), (5, 1), (6, 1), (7, 1))


def split(value):
    high = value.astype(BF16)
    return high, (value - high.astype(F32)).astype(BF16)


def dot(left, right):
    return jnp.dot(left, right, preferred_element_type=F32)


def product(left, right):
    return dot(left[0], right[0]) + (dot(left[0], right[1]) + dot(left[1], right[0]))


def kernel(pivot_ref, col_ref, row_ref, trail_ref, out_ref, piv, rb, cb, trail, f_a, f_b, h_a, h_b, h_inv1, h_n, h_ll, h_inv2, h_y,
           loc, ps, pr, xs, xr, zs, zr, bs, br, rs, rr, inz, inx, iny, ins):
    y = lax.axis_index("row")
    col = lax.axis_index("col")
    c = lax.rem(col, 2)
    x = lax.rem(col // 2, N)
    z = col // (2 * N)
    p = jnp.where(c == 0, z, x)
    q = jnp.where(c == 0, x, z)

    def column(z_, x_, c_):
        return (z_ * N + x_) * 2 + c_

    def first(y_, z_, x_, c_):
        return jnp.where((y_ == 0) & (z_ == 0) & (x_ == 0) & (c_ == 0), 100, 0)

    def ringed(v):
        return 2 * jnp.minimum(v, N - v) - jnp.where(v < N // 2, 1, 0)

    mine = first(y, z, x, c)
    partners = []
    zp, xp, yp = [], [], []
    for k in range(N):
        zp.append((y, column(k, x, c)))
        partners.append((zp[k], z != k, k + first(y, k, x, c) > z + mine, inz.at[z], inz.at[k]))
    for o in range(1, N):
        k = lax.rem(x + o, N)
        xp.append((y, column(z, k, c)))
        partners.append((xp[-1], None, ringed(k) + first(y, z, k, c) > ringed(x) + mine, inx.at[x], inx.at[k]))
    for k, off in enumerate((1, N - 1, 2, N - 2)):
        other = lax.rem(y + off, N)
        yp.append((other, col))
        partners.append((yp[k], None, ringed(other) + first(other, z, x, c) > ringed(y) + mine, iny.at[k ^ 1], iny.at[k]))
    sib = (y, column(z, x, 1 - c))
    partners.append((sib, None, (c == 1), ins.at[0], ins.at[0]))

    def both(a, b):
        return b if a is None else a & b

    local = []
    for k, (down, right) in enumerate(((0, 0), (0, 1), (1, 0), (1, 1))):
        part = (pl.ds(down * B, B), pl.ds(right * B, B))
        local.append(pltpu.make_async_copy(pivot_ref.at[part], piv.at[part], loc.at[k]))
    own_c = pltpu.make_async_copy(col_ref, cb.at[c, p, q], loc.at[4])
    own_r = pltpu.make_async_copy(row_ref, rb.at[y], loc.at[5])
    own_t = pltpu.make_async_copy(trail_ref, trail, loc.at[6])
    own_c.start()
    local[0].start()

    barrier = pltpu.get_barrier_semaphore()
    count = jnp.int32(0)
    for dev, there, later, _, _ in partners:
        earlier = both(there, jnp.logical_not(later))
        count = count + earlier.astype(jnp.int32)

        @pl.when(both(there, later))
        def _():
            pl.semaphore_signal(barrier, inc=1, device_id=dev, device_id_type=MESH)

    @pl.when(count > 0)
    def _():
        pl.semaphore_wait(barrier, count)

    def remote(src, dst, send, recv, dev):
        return pltpu.make_async_remote_copy(src_ref=src, dst_ref=dst, send_sem=send, recv_sem=recv, device_id=dev, device_id_type=MESH)

    def first_z(k):
        return remote(col_ref, cb.at[0, z, x], ps.at[k], pr.at[z], zp[k])

    def first_z_wait(k):
        remote(col_ref, cb.at[0, k, x], ps.at[k], pr.at[k], zp[k]).wait_recv()

    def first_x(o):
        return remote(col_ref, cb.at[1, x, z], ps.at[o], pr.at[o], xp[o - 1])

    def first_x_wait(o):
        remote(col_ref, cb.at[1, lax.rem(x + N - o, N), z], ps.at[o], pr.at[o], xp[o - 1]).wait_recv()

    for k in range(N):
        _, there, later, _, _ = partners[k]

        @pl.when((c == 0) & there & jnp.logical_not(later))
        def _():
            first_z(k).start()

    for o in (4, 3, 5, 2, 6, 1, 7):
        @pl.when((c == 1) & jnp.logical_not(partners[N + o - 1][2]))
        def _():
            first_x(o).start()

    for dev, there, later, theirs, _ in partners:
        @pl.when(both(there, jnp.logical_not(later)))
        def _():
            pl.semaphore_signal(theirs, inc=1, device_id=dev, device_id_type=MESH)

    def admit(i):
        _, there, later, _, own = partners[i]

        @pl.when(both(there, later))
        def _():
            pl.semaphore_wait(own, 1)

    for k in range(1, 4):
        local[k].start()
    own_r.start()
    own_t.start()

    half = B // 8

    def r_copy(k):
        src_y = lax.rem(y + (0, 0, 0, 0, N - 2, 2, N - 2, 2)[k], N)
        dev = yp[(0, 1, 2, 3, 0, 1, 2, 3)[k]]
        if k < 4:
            src, dst = row_ref, rb.at[y]
        elif k < 6:
            src = dst = rb.at[src_y]
        else:
            src = dst = rb.at[src_y, pl.ds((k - 6) * half, half)]
        return remote(src, dst, rs.at[k], rr.at[k], dev)

    def r_wait(k):
        at = lax.rem(y + (N - 1, 1, N - 2, 2, N - 3, 3, N - 4, 4)[k], N)
        ref = rb.at[at] if k < 6 else rb.at[at, pl.ds((k - 6) * half, half)]
        remote(ref, ref, rs.at[k], rr.at[k], yp[0]).wait_recv()

    for k in (2, 3, 0, 1):
        admit(2 * N - 1 + k)
        r_copy(k).start()
    admit(2 * N + 3)

    eye = (lax.broadcasted_iota(jnp.int32, (B, B), 0) == lax.broadcasted_iota(jnp.int32, (B, B), 1)).astype(F32)

    def load(ref):
        return ref[0], ref[1]

    def store(ref, value):
        ref[0], ref[1] = split(value)

    local[0].wait()
    e = eye - piv[:B, :B]
    f_a[...] = e
    store(h_a, e)
    square = product(load(h_a), load(h_a))
    f_b[...] = square
    store(h_b, square)
    store(h_inv1, eye + f_a[...] + f_b[...] + product(load(h_a), load(h_b)))
    local[1].wait()
    store(h_n, product(load(h_inv1), split(piv[:B, B:])))

    @pl.when(c == 1)
    def _():
        for o in (1, 7, 2, 6, 3, 5, 4):
            _, _, later, _, own = partners[N + o - 1]

            @pl.when(later)
            def _():
                pl.semaphore_wait(own, 1)
                first_x(o).start()

    local[2].wait()
    local[3].wait()
    store(h_ll, piv[B:, :B])
    e = eye - piv[B:, B:] + product(load(h_ll), load(h_n))
    f_a[...] = e
    store(h_a, e)

    def second_z(k):
        ref = cb.at[1, :, z]
        return remote(ref, ref, zs.at[k], zr.at[z], zp[k])

    def second_z_wait(k):
        ref = cb.at[1, :, k]
        remote(ref, ref, zs.at[k], zr.at[k], zp[k]).wait_recv()

    own_c.wait()

    @pl.when(c == 1)
    def _():
        for o in (1, 7, 2, 6, 3, 5, 4):
            first_x_wait(o)
        for k in range(N):
            _, there, later, _, _ = partners[k]

            @pl.when(there & jnp.logical_not(later))
            def _():
                second_z(k).start()

    r_wait(2)
    r_copy(4).start()
    r_copy(6).start()
    r_wait(3)
    r_copy(5).start()
    r_copy(7).start()
    def second_x(g, o):
        z0, n = GROUPS[g]
        ref = cb.at[0, pl.ds(z0, n), x]
        return remote(ref, ref, xs.at[g, o - 1], xr.at[g, o - 1], xp[o - 1])

    def second_x_wait(g, o):
        z0, n = GROUPS[g]
        ref = cb.at[0, pl.ds(z0, n), lax.rem(x + N - o, N)]
        remote(ref, ref, xs.at[g, o - 1], xr.at[g, o - 1], xp[o - 1]).wait_recv()

    def pass_on(g):
        z0, n = GROUPS[g]

        @pl.when(c == 0)
        def _():
            for k in range(z0, z0 + n):
                _, there, later, _, own = partners[k]

                @pl.when(there & later)
                def _():
                    pl.semaphore_wait(own, 1)
                    first_z(k).start()

                @pl.when(there)
                def _():
                    first_z_wait(k)

            for o in (4, 3, 5, 2, 6, 1, 7):
                second_x(g, o).start()

        @pl.when(c == 1)
        def _():
            for k in range(z0, z0 + n):
                _, there, later, _, own = partners[k]

                @pl.when(there & later)
                def _():
                    pl.semaphore_wait(own, 1)
                    second_z(k).start()

    @pl.when(c == 0)
    def _():
        for k in range(N - 1):
            admit(N + k)

    pass_on(0)
    pass_on(1)
    square = product(load(h_a), load(h_a))
    f_b[...] = square
    store(h_b, square)
    store(h_inv2, eye + f_a[...] + f_b[...] + product(load(h_a), load(h_b)))

    for g in range(2, len(GROUPS)):
        pass_on(g)

    def third(g, core):
        z0, n = GROUPS[g]
        ref = cb.at[0, pl.ds(z0, n)] if core == 0 else cb.at[1, :, pl.ds(z0, n)]
        return remote(ref, ref, bs.at[g], br.at[g], sib)

    def share(g):
        z0, n = GROUPS[g]

        @pl.when(c == 0)
        def _():
            for o in (1, 7, 2, 6, 3, 5, 4):
                second_x_wait(g, o)
            third(g, 0).start()

        @pl.when(c == 1)
        def _():
            for k in range(z0, z0 + n):
                @pl.when(z != k)
                def _():
                    second_z_wait(k)
            third(g, 1).start()

    share(0)
    share(1)
    own_r.wait()
    for k in (0, 1, 4, 5, 6, 7):
        r_wait(k)
    first_rows = rb[0:4].reshape(B, 2 * 128)
    second_rows = rb[4:8].reshape(B, 2 * 128)
    u = product(load(h_inv1), split(first_rows))
    rest = second_rows - product(load(h_ll), split(u))
    share(2)
    y_two = split(product(load(h_inv2), split(rest)))
    h_y[0, B:], h_y[1, B:] = y_two
    h_y[0, :B], h_y[1, :B] = split(u - product(load(h_n), y_two))
    own_t.wait()

    def eliminate(g):
        z0, n = GROUPS[g]
        k0, kn = z0 * 128, n * 128

        @pl.when(c == 0)
        def _():
            third(g, 1).wait_recv()

        @pl.when(c == 1)
        def _():
            third(g, 0).wait_recv()

        blocks = []
        for a in range(z0, z0 + n):
            for b in range(N):
                blocks += [cb[0, a, b], cb[1, b, a]]
        left = jnp.concatenate(blocks, axis=0).T
        return product(split(left), (h_y[0, k0:k0 + kn], h_y[1, k0:k0 + kn]))

    trail[...] = trail[...] - eliminate(0)
    share(3)
    trail[...] = trail[...] - eliminate(1)
    share(4)
    trail[...] = trail[...] - eliminate(2)
    share(5)
    trail[...] = trail[...] - eliminate(3)
    trail[...] = trail[...] - eliminate(4)
    out_ref[...] = trail[...] - eliminate(5)

    for k in range(8):
        r_copy(k).wait_send()

    @pl.when(c == 0)
    def _():
        for k in range(N):
            @pl.when(z != k)
            def _():
                first_z(k).wait_send()

        for g in range(len(GROUPS)):
            for o in range(1, N):
                second_x(g, o).wait_send()
            third(g, 0).wait_send()

    @pl.when(c == 1)
    def _():
        for o in range(1, N):
            first_x(o).wait_send()
        for k in range(N):
            @pl.when(z != k)
            def _():
                second_z(k).wait_send()

        for g in range(len(GROUPS)):
            third(g, 1).wait_send()


def local_step(pivot, col_panel, row_panel, trailing):
    pair = pltpu.VMEM((2, B, B), BF16)
    return pl.pallas_call(
        kernel,
        out_shape=jax.ShapeDtypeStruct(trailing.shape, F32),
        in_specs=[pl.BlockSpec(memory_space=pl.ANY)] * 4,
        out_specs=pl.BlockSpec(memory_space=pltpu.VMEM),
        scratch_shapes=[
            pltpu.VMEM((2 * B, 2 * B), F32),
            pltpu.VMEM((N, 128, 256), F32),
            pltpu.VMEM((2, N, N, 8, B), F32),
            pltpu.VMEM((B, 256), F32),
            pltpu.VMEM((B, B), F32),
            pltpu.VMEM((B, B), F32),
            pair, pair, pair, pair, pair, pair,
            pltpu.VMEM((2, 2 * B, 256), BF16),
            pltpu.SemaphoreType.DMA((7,)),
            pltpu.SemaphoreType.DMA((N,)),
            pltpu.SemaphoreType.DMA((N,)),
            pltpu.SemaphoreType.DMA((len(GROUPS), N)),
            pltpu.SemaphoreType.DMA((len(GROUPS), N)),
            pltpu.SemaphoreType.DMA((N,)),
            pltpu.SemaphoreType.DMA((N,)),
            pltpu.SemaphoreType.DMA((len(GROUPS),)),
            pltpu.SemaphoreType.DMA((len(GROUPS),)),
            pltpu.SemaphoreType.DMA((8,)),
            pltpu.SemaphoreType.DMA((8,)),
            pltpu.SemaphoreType.REGULAR((N,)),
            pltpu.SemaphoreType.REGULAR((N,)),
            pltpu.SemaphoreType.REGULAR((4,)),
            pltpu.SemaphoreType.REGULAR((1,)),
        ],
        compiler_params=pltpu.CompilerParams(collective_id=0, has_side_effects=True, vmem_limit_bytes=56 << 20),
        name="eliminate",
    )(pivot, col_panel.T, row_panel, trailing)


def solution(mesh):
    return jax.shard_map(
        local_step,
        mesh=mesh,
        in_specs=(P(), P("row", "col"), P("row", "col"), P("row", "col")),
        out_specs=P("row", "col"),
        check_vma=False,
    )
```

```python
import jax
import jax.numpy as jnp
from jax import lax
from jax.experimental import pallas as pl
from jax.experimental.pallas import tpu as pltpu
from jax.sharding import PartitionSpec as P

B = 512
N = 8
MESH = pl.DeviceIdType.MESH
F32 = jnp.float32
BF16 = jnp.bfloat16
GROUPS = ((0, 2), (2, 2), (4, 1), (5, 1), (6, 1), (7, 1))


def split(value):
    high = value.astype(BF16)
    return high, (value - high.astype(F32)).astype(BF16)


def dot(left, right):
    return jnp.dot(left, right, preferred_element_type=F32)


def product(left, right):
    return dot(left[0], right[0]) + (dot(left[0], right[1]) + dot(left[1], right[0]))


def kernel(pivot_ref, col_ref, row_ref, trail_ref, out_ref, piv, rb, cb, trail, f_a, f_b, h_a, h_b, h_inv1, h_n, h_ll, h_inv2, h_y,
           loc, ps, pr, xs, xr, zs, zr, bs, br, rs, rr, inz, inx, iny, ins):
    y = lax.axis_index("row")
    col = lax.axis_index("col")
    c = lax.rem(col, 2)
    x = lax.rem(col // 2, N)
    z = col // (2 * N)
    p = jnp.where(c == 0, z, x)
    q = jnp.where(c == 0, x, z)

    def column(z_, x_, c_):
        return (z_ * N + x_) * 2 + c_

    def first(y_, z_, x_, c_):
        return jnp.where((y_ == 0) & (z_ == 0) & (x_ == 0) & (c_ == 0), 100, 0)

    def ringed(v):
        return 2 * jnp.minimum(v, N - v) - jnp.where(v < N // 2, 1, 0)

    mine = first(y, z, x, c)
    partners = []
    zp, xp, yp = [], [], []
    for k in range(N):
        zp.append((y, column(k, x, c)))
        apart = lax.rem(z + N - k, N)
        partners.append((zp[k], (z != k) & ((c == 0) | (apart == 1) | (apart == N - 1)), k + first(y, k, x, c) > z + mine, inz.at[z], inz.at[k]))
    for o in range(1, N):
        k = lax.rem(x + o, N)
        xp.append((y, column(z, k, c)))
        partners.append((xp[-1], None, ringed(k) + first(y, z, k, c) > ringed(x) + mine, inx.at[x], inx.at[k]))
    for k, off in enumerate((1, N - 1, 2, N - 2)):
        other = lax.rem(y + off, N)
        yp.append((other, col))
        partners.append((yp[k], None, ringed(other) + first(other, z, x, c) > ringed(y) + mine, iny.at[k ^ 1], iny.at[k]))
    sib = (y, column(z, x, 1 - c))
    partners.append((sib, None, (c == 1), ins.at[0], ins.at[0]))

    def both(a, b):
        return b if a is None else a & b

    local = []
    for k, (down, right) in enumerate(((0, 0), (0, 1), (1, 0), (1, 1))):
        part = (pl.ds(down * B, B), pl.ds(right * B, B))
        local.append(pltpu.make_async_copy(pivot_ref.at[part], piv.at[part], loc.at[k]))
    own_c = pltpu.make_async_copy(col_ref, cb.at[c, p, q], loc.at[4])
    own_r = pltpu.make_async_copy(row_ref, rb.at[y], loc.at[5])
    own_t = pltpu.make_async_copy(trail_ref, trail, loc.at[6])
    own_c.start()
    local[0].start()

    barrier = pltpu.get_barrier_semaphore()
    count = jnp.int32(0)
    for dev, there, later, _, _ in partners:
        earlier = both(there, jnp.logical_not(later))
        count = count + earlier.astype(jnp.int32)

        @pl.when(both(there, later))
        def _():
            pl.semaphore_signal(barrier, inc=1, device_id=dev, device_id_type=MESH)

    @pl.when(count > 0)
    def _():
        pl.semaphore_wait(barrier, count)

    def remote(src, dst, send, recv, dev):
        return pltpu.make_async_remote_copy(src_ref=src, dst_ref=dst, send_sem=send, recv_sem=recv, device_id=dev, device_id_type=MESH)

    def first_z(k):
        return remote(col_ref, cb.at[0, z, x], ps.at[k], pr.at[z], zp[k])

    def first_z_wait(k):
        remote(col_ref, cb.at[0, k, x], ps.at[k], pr.at[k], zp[k]).wait_recv()

    def first_x(o):
        return remote(col_ref, cb.at[1, x, z], ps.at[o], pr.at[o], xp[o - 1])

    def first_x_wait(o):
        remote(col_ref, cb.at[1, lax.rem(x + N - o, N), z], ps.at[o], pr.at[o], xp[o - 1]).wait_recv()

    for k in range(N):
        _, there, later, _, _ = partners[k]

        @pl.when((c == 0) & there & jnp.logical_not(later))
        def _():
            first_z(k).start()

    for o in (4, 3, 5, 2, 6, 1, 7):
        @pl.when((c == 1) & jnp.logical_not(partners[N + o - 1][2]))
        def _():
            first_x(o).start()

    for dev, there, later, theirs, _ in partners:
        @pl.when(both(there, jnp.logical_not(later)))
        def _():
            pl.semaphore_signal(theirs, inc=1, device_id=dev, device_id_type=MESH)

    def admit(i):
        _, there, later, _, own = partners[i]

        @pl.when(both(there, later))
        def _():
            pl.semaphore_wait(own, 1)

    for k in range(1, 4):
        local[k].start()
    own_r.start()
    own_t.start()

    half = B // 8

    def r_copy(k):
        src_y = lax.rem(y + (0, 0, 0, 0, N - 2, 2, N - 2, 2)[k], N)
        dev = yp[(0, 1, 2, 3, 0, 1, 2, 3)[k]]
        if k < 4:
            src, dst = row_ref, rb.at[y]
        elif k < 6:
            src = dst = rb.at[src_y]
        else:
            src = dst = rb.at[src_y, pl.ds((k - 6) * half, half)]
        return remote(src, dst, rs.at[k], rr.at[k], dev)

    def r_wait(k):
        at = lax.rem(y + (N - 1, 1, N - 2, 2, N - 3, 3, N - 4, 4)[k], N)
        ref = rb.at[at] if k < 6 else rb.at[at, pl.ds((k - 6) * half, half)]
        remote(ref, ref, rs.at[k], rr.at[k], yp[0]).wait_recv()

    for k in (2, 3, 0, 1):
        admit(2 * N - 1 + k)
        r_copy(k).start()
    admit(2 * N + 3)

    eye = (lax.broadcasted_iota(jnp.int32, (B, B), 0) == lax.broadcasted_iota(jnp.int32, (B, B), 1)).astype(F32)

    def load(ref):
        return ref[0], ref[1]

    def store(ref, value):
        ref[0], ref[1] = split(value)

    local[0].wait()
    e = eye - piv[:B, :B]
    f_a[...] = e
    store(h_a, e)
    square = product(load(h_a), load(h_a))
    f_b[...] = square
    store(h_b, square)
    store(h_inv1, eye + f_a[...] + f_b[...] + product(load(h_a), load(h_b)))
    local[1].wait()
    store(h_n, product(load(h_inv1), split(piv[:B, B:])))

    @pl.when(c == 1)
    def _():
        for o in (1, 7, 2, 6, 3, 5, 4):
            _, _, later, _, own = partners[N + o - 1]

            @pl.when(later)
            def _():
                pl.semaphore_wait(own, 1)
                first_x(o).start()

    local[2].wait()
    local[3].wait()
    store(h_ll, piv[B:, :B])
    e = eye - piv[B:, B:] + product(load(h_ll), load(h_n))
    f_a[...] = e
    store(h_a, e)

    def slot_of(step, way):
        return lax.rem(z + (N - step if way == 0 else step), N)

    def ring_ref(slot, step, way):
        return cb.at[1, :, slot] if step < 4 else cb.at[1, pl.ds(4 * way, 4), slot]

    def ring(way, step):
        ref = ring_ref(slot_of(step - 1, way), step, way)
        dev = (y, column(lax.rem(z + (1, N - 1)[way], N), x, c))
        at = 4 * way + step - 1
        return remote(ref, ref, zs.at[at], zr.at[at], dev)

    def ring_step(way, step):
        ref = ring_ref(slot_of(step, way), step, way)
        at = 4 * way + step - 1
        remote(ref, ref, zs.at[at], zr.at[at], sib).wait_recv()
        if step < 4:
            ring(way, step + 1).start()

    def third_x(g):
        z0, n = GROUPS[g]
        ref = cb.at[0, pl.ds(z0, n)]
        return remote(ref, ref, bs.at[g], br.at[g], sib)

    def third_z(k):
        ref = cb.at[1, :, k]
        return remote(ref, ref, bs.at[k], br.at[k], sib)

    own_c.wait()

    @pl.when(c == 1)
    def _():
        for o in (1, 7, 2, 6, 3, 5, 4):
            first_x_wait(o)
        @pl.when(z != N - 1)
        def _():
            pl.semaphore_wait(inz.at[z + 1], 1)

        ring(0, 1).start()

        @pl.when(z != 0)
        def _():
            ring(1, 1).start()

        third_z(z).start()

    r_wait(2)
    r_copy(4).start()
    r_copy(6).start()
    r_wait(3)
    r_copy(5).start()
    r_copy(7).start()
    def second_x(g, o):
        z0, n = GROUPS[g]
        ref = cb.at[0, pl.ds(z0, n), x]
        return remote(ref, ref, xs.at[g, o - 1], xr.at[g, o - 1], xp[o - 1])

    def second_x_wait(g, o):
        z0, n = GROUPS[g]
        ref = cb.at[0, pl.ds(z0, n), lax.rem(x + N - o, N)]
        remote(ref, ref, xs.at[g, o - 1], xr.at[g, o - 1], xp[o - 1]).wait_recv()

    def pass_on(g):
        z0, n = GROUPS[g]

        @pl.when(c == 0)
        def _():
            for k in range(z0, z0 + n):
                _, there, later, _, own = partners[k]

                @pl.when(there & later)
                def _():
                    pl.semaphore_wait(own, 1)
                    first_z(k).start()

                @pl.when(there)
                def _():
                    first_z_wait(k)

            for o in (4, 3, 5, 2, 6, 1, 7):
                second_x(g, o).start()

    @pl.when(c == 0)
    def _():
        for k in range(N - 1):
            admit(N + k)

    pass_on(0)
    pass_on(1)
    square = product(load(h_a), load(h_a))
    f_b[...] = square
    store(h_b, square)
    store(h_inv2, eye + f_a[...] + f_b[...] + product(load(h_a), load(h_b)))

    for g in range(2, len(GROUPS)):
        pass_on(g)

    @pl.when(c == 1)
    def _():
        @pl.when(z == 0)
        def _():
            pl.semaphore_wait(inz.at[N - 1], 1)
            ring(1, 1).start()

        for step in range(1, 4):
            @pl.when(z >= 4 + step)
            def _():
                ring_step(0, step)

        for step in range(1, 5):
            ring_step(1, step)
            if step < 4:
                third_z(slot_of(step, 1)).start()

    def share(g):
        @pl.when(c == 0)
        def _():
            for o in (1, 7, 2, 6, 3, 5, 4):
                second_x_wait(g, o)
            third_x(g).start()

    share(0)
    share(1)
    own_r.wait()
    for k in (0, 1, 4, 5, 6, 7):
        r_wait(k)
    first_rows = rb[0:4].reshape(B, 2 * 128)
    second_rows = rb[4:8].reshape(B, 2 * 128)
    u = product(load(h_inv1), split(first_rows))
    rest = second_rows - product(load(h_ll), split(u))
    share(2)
    y_two = split(product(load(h_inv2), split(rest)))
    h_y[0, B:], h_y[1, B:] = y_two
    h_y[0, :B], h_y[1, :B] = split(u - product(load(h_n), y_two))
    own_t.wait()
    for g in range(3, len(GROUPS)):
        share(g)

    @pl.when(c == 1)
    def _():
        for step in range(1, 5):
            @pl.when(z < 4 + step)
            def _():
                ring_step(0, step)

            third_z(slot_of(step, 0)).start()
        for g in range(len(GROUPS)):
            third_x(g).wait_recv()

    @pl.when(c == 0)
    def _():
        for k in range(N):
            third_z(k).wait_recv()

    def eliminate(z0, n):
        k0, kn = z0 * 128, n * 128
        blocks = []
        for a in range(z0, z0 + n):
            for b in range(N):
                blocks += [cb[0, a, b], cb[1, b, a]]
        left = jnp.concatenate(blocks, axis=0).T
        return product(split(left), (h_y[0, k0:k0 + kn], h_y[1, k0:k0 + kn]))

    trail[...] = trail[...] - eliminate(0, 4)
    out_ref[...] = trail[...] - eliminate(4, 4)

    for k in range(8):
        r_copy(k).wait_send()

    @pl.when(c == 0)
    def _():
        for k in range(N):
            @pl.when(z != k)
            def _():
                first_z(k).wait_send()

        for g in range(len(GROUPS)):
            for o in range(1, N):
                second_x(g, o).wait_send()
            third_x(g).wait_send()

    @pl.when(c == 1)
    def _():
        for o in range(1, N):
            first_x(o).wait_send()
        for step in range(1, 5):
            ring(0, step).wait_send()
            ring(1, step).wait_send()
        for k in range(N):
            third_z(k).wait_send()


def local_step(pivot, col_panel, row_panel, trailing):
    pair = pltpu.VMEM((2, B, B), BF16)
    return pl.pallas_call(
        kernel,
        out_shape=jax.ShapeDtypeStruct(trailing.shape, F32),
        in_specs=[pl.BlockSpec(memory_space=pl.ANY)] * 4,
        out_specs=pl.BlockSpec(memory_space=pltpu.VMEM),
        scratch_shapes=[
            pltpu.VMEM((2 * B, 2 * B), F32),
            pltpu.VMEM((N, 128, 256), F32),
            pltpu.VMEM((2, N, N, 8, B), F32),
            pltpu.VMEM((B, 256), F32),
            pltpu.VMEM((B, B), F32),
            pltpu.VMEM((B, B), F32),
            pair, pair, pair, pair, pair, pair,
            pltpu.VMEM((2, 2 * B, 256), BF16),
            pltpu.SemaphoreType.DMA((7,)),
            pltpu.SemaphoreType.DMA((N,)),
            pltpu.SemaphoreType.DMA((N,)),
            pltpu.SemaphoreType.DMA((len(GROUPS), N)),
            pltpu.SemaphoreType.DMA((len(GROUPS), N)),
            pltpu.SemaphoreType.DMA((N,)),
            pltpu.SemaphoreType.DMA((N,)),
            pltpu.SemaphoreType.DMA((N,)),
            pltpu.SemaphoreType.DMA((N,)),
            pltpu.SemaphoreType.DMA((8,)),
            pltpu.SemaphoreType.DMA((8,)),
            pltpu.SemaphoreType.REGULAR((N,)),
            pltpu.SemaphoreType.REGULAR((N,)),
            pltpu.SemaphoreType.REGULAR((4,)),
            pltpu.SemaphoreType.REGULAR((1,)),
        ],
        compiler_params=pltpu.CompilerParams(collective_id=0, has_side_effects=True, vmem_limit_bytes=56 << 20),
        name="eliminate",
    )(pivot, col_panel.T, row_panel, trailing)


def solution(mesh):
    return jax.shard_map(
        local_step,
        mesh=mesh,
        in_specs=(P(), P("row", "col"), P("row", "col"), P("row", "col")),
        out_specs=P("row", "col"),
        check_vma=False,
    )
```

```python
import jax
import jax.numpy as jnp
from jax import lax
from jax.experimental import pallas as pl
from jax.experimental.pallas import tpu as pltpu
from jax.sharding import PartitionSpec as P

B = 512
N = 8
MESH = pl.DeviceIdType.MESH
F32 = jnp.float32
BF16 = jnp.bfloat16
GROUPS = ((0, 2), (2, 2), (4, 1), (5, 1), (6, 1), (7, 1))


def split(value):
    high = value.astype(BF16)
    return high, (value - high.astype(F32)).astype(BF16)


def dot(left, right):
    return jnp.dot(left, right, preferred_element_type=F32)


def product(left, right):
    return dot(left[0], right[0]) + (dot(left[0], right[1]) + dot(left[1], right[0]))


def kernel(pivot_ref, col_ref, row_ref, trail_ref, out_ref, piv, rb, cb, trail, f_a, f_b, h_a, h_b, h_inv1, h_n, h_ll, h_inv2, h_y,
           loc, ps, pr, xs, xr, zs, zr, bs, br, rs, rr, inz, inx, iny, ins):
    y = lax.axis_index("row")
    col = lax.axis_index("col")
    c = lax.rem(col, 2)
    x = lax.rem(col // 2, N)
    z = col // (2 * N)
    p = jnp.where(c == 0, z, x)
    q = jnp.where(c == 0, x, z)

    def column(z_, x_, c_):
        return (z_ * N + x_) * 2 + c_

    def first(y_, z_, x_, c_):
        return jnp.where((y_ == 0) & (z_ == 0) & (x_ == 0) & (c_ == 0), 100, 0)

    def ringed(v):
        return 2 * jnp.minimum(v, N - v) - jnp.where(v < N // 2, 1, 0)

    mine = first(y, z, x, c)
    partners = []
    zp, xp, yp = [], [], []
    for k in range(N):
        zp.append((y, column(k, x, c)))
        partners.append((zp[k], z != k, k + first(y, k, x, c) > z + mine, inz.at[z], inz.at[k]))
    for o in range(1, N):
        k = lax.rem(x + o, N)
        xp.append((y, column(z, k, c)))
        partners.append((xp[-1], None, ringed(k) + first(y, z, k, c) > ringed(x) + mine, inx.at[x], inx.at[k]))
    for k, off in enumerate((1, N - 1, 2, N - 2)):
        other = lax.rem(y + off, N)
        yp.append((other, col))
        partners.append((yp[k], None, ringed(other) + first(other, z, x, c) > ringed(y) + mine, iny.at[k ^ 1], iny.at[k]))
    sib = (y, column(z, x, 1 - c))
    partners.append((sib, None, (c == 1), ins.at[0], ins.at[0]))

    def both(a, b):
        return b if a is None else a & b

    local = []
    for k, (down, right) in enumerate(((0, 0), (0, 1), (1, 0), (1, 1))):
        part = (pl.ds(down * B, B), pl.ds(right * B, B))
        local.append(pltpu.make_async_copy(pivot_ref.at[part], piv.at[part], loc.at[k]))
    own_c = pltpu.make_async_copy(col_ref, cb.at[c, p, q], loc.at[4])
    own_r = pltpu.make_async_copy(row_ref, rb.at[y], loc.at[5])
    own_t = pltpu.make_async_copy(trail_ref, trail, loc.at[6])
    own_c.start()
    local[0].start()

    barrier = pltpu.get_barrier_semaphore()
    count = jnp.int32(0)
    for dev, there, later, _, _ in partners:
        earlier = both(there, jnp.logical_not(later))
        count = count + earlier.astype(jnp.int32)

        @pl.when(both(there, later))
        def _():
            pl.semaphore_signal(barrier, inc=1, device_id=dev, device_id_type=MESH)

    @pl.when(count > 0)
    def _():
        pl.semaphore_wait(barrier, count)

    def remote(src, dst, send, recv, dev):
        return pltpu.make_async_remote_copy(src_ref=src, dst_ref=dst, send_sem=send, recv_sem=recv, device_id=dev, device_id_type=MESH)

    def first_z(k):
        return remote(col_ref, cb.at[0, z, x], ps.at[k], pr.at[z], zp[k])

    def first_z_wait(k):
        remote(col_ref, cb.at[0, k, x], ps.at[k], pr.at[k], zp[k]).wait_recv()

    def first_x(o):
        return remote(col_ref, cb.at[1, x, z], ps.at[o], pr.at[o], xp[o - 1])

    def first_x_wait(o):
        remote(col_ref, cb.at[1, lax.rem(x + N - o, N), z], ps.at[o], pr.at[o], xp[o - 1]).wait_recv()

    for k in range(N):
        _, there, later, _, _ = partners[k]

        @pl.when((c == 0) & there & jnp.logical_not(later))
        def _():
            first_z(k).start()

    for o in (4, 3, 5, 2, 6, 1, 7):
        @pl.when((c == 1) & jnp.logical_not(partners[N + o - 1][2]))
        def _():
            first_x(o).start()

    for dev, there, later, theirs, _ in partners:
        @pl.when(both(there, jnp.logical_not(later)))
        def _():
            pl.semaphore_signal(theirs, inc=1, device_id=dev, device_id_type=MESH)

    def admit(i):
        _, there, later, _, own = partners[i]

        @pl.when(both(there, later))
        def _():
            pl.semaphore_wait(own, 1)

    for k in range(1, 4):
        local[k].start()
    own_r.start()
    own_t.start()

    half = B // 8

    def r_copy(k):
        src_y = lax.rem(y + (0, 0, 0, 0, N - 2, 2, N - 2, 2)[k], N)
        dev = yp[(0, 1, 2, 3, 0, 1, 2, 3)[k]]
        if k < 4:
            src, dst = row_ref, rb.at[y]
        elif k < 6:
            src = dst = rb.at[src_y]
        else:
            src = dst = rb.at[src_y, pl.ds((k - 6) * half, half)]
        return remote(src, dst, rs.at[k], rr.at[k], dev)

    def r_wait(k):
        at = lax.rem(y + (N - 1, 1, N - 2, 2, N - 3, 3, N - 4, 4)[k], N)
        ref = rb.at[at] if k < 6 else rb.at[at, pl.ds((k - 6) * half, half)]
        remote(ref, ref, rs.at[k], rr.at[k], yp[0]).wait_recv()

    for k in (2, 3, 0, 1):
        admit(2 * N - 1 + k)
        r_copy(k).start()
    admit(2 * N + 3)

    eye = (lax.broadcasted_iota(jnp.int32, (B, B), 0) == lax.broadcasted_iota(jnp.int32, (B, B), 1)).astype(F32)

    def load(ref):
        return ref[0], ref[1]

    def store(ref, value):
        ref[0], ref[1] = split(value)

    local[0].wait()
    e = eye - piv[:B, :B]
    f_a[...] = e
    store(h_a, e)
    square = product(load(h_a), load(h_a))
    f_b[...] = square
    store(h_b, square)
    store(h_inv1, eye + f_a[...] + f_b[...] + product(load(h_a), load(h_b)))
    local[1].wait()
    store(h_n, product(load(h_inv1), split(piv[:B, B:])))

    @pl.when(c == 1)
    def _():
        for o in (1, 7, 2, 6, 3, 5, 4):
            _, _, later, _, own = partners[N + o - 1]

            @pl.when(later)
            def _():
                pl.semaphore_wait(own, 1)
                first_x(o).start()

    local[2].wait()
    local[3].wait()
    store(h_ll, piv[B:, :B])
    e = eye - piv[B:, B:] + product(load(h_ll), load(h_n))
    f_a[...] = e
    store(h_a, e)

    def second_z(k):
        ref = cb.at[1, :, z]
        return remote(ref, ref, zs.at[k], zr.at[z], zp[k])

    def second_z_wait(k):
        ref = cb.at[1, :, k]
        remote(ref, ref, zs.at[k], zr.at[k], zp[k]).wait_recv()

    own_c.wait()

    @pl.when(c == 1)
    def _():
        for o in (1, 7, 2, 6, 3, 5, 4):
            first_x_wait(o)
        for k in range(N):
            _, there, later, _, _ = partners[k]

            @pl.when(there & jnp.logical_not(later))
            def _():
                second_z(k).start()

    r_wait(2)
    r_copy(4).start()
    r_copy(6).start()
    r_wait(3)
    r_copy(5).start()
    r_copy(7).start()
    def second_x(g, o):
        z0, n = GROUPS[g]
        ref = cb.at[0, pl.ds(z0, n), x]
        return remote(ref, ref, xs.at[g, o - 1], xr.at[g, o - 1], xp[o - 1])

    def second_x_wait(g, o):
        z0, n = GROUPS[g]
        ref = cb.at[0, pl.ds(z0, n), lax.rem(x + N - o, N)]
        remote(ref, ref, xs.at[g, o - 1], xr.at[g, o - 1], xp[o - 1]).wait_recv()

    def pass_on(g):
        z0, n = GROUPS[g]

        @pl.when(c == 0)
        def _():
            for k in range(z0, z0 + n):
                _, there, later, _, own = partners[k]

                @pl.when(there & later)
                def _():
                    pl.semaphore_wait(own, 1)
                    first_z(k).start()

                @pl.when(there)
                def _():
                    first_z_wait(k)

            for o in (4, 3, 5, 2, 6, 1, 7):
                if g == 0:
                    @pl.when(jnp.logical_not(partners[N + o - 1][2]))
                    def _():
                        second_x(g, o).start()
                else:
                    second_x(g, o).start()

            if g == 0:
                for o in (1, 7, 2, 6, 3, 5, 4):
                    @pl.when(partners[N + o - 1][2])
                    def _():
                        pl.semaphore_wait(partners[N + o - 1][4], 1)
                        second_x(g, o).start()

        @pl.when(c == 1)
        def _():
            for k in range(z0, z0 + n):
                _, there, later, _, own = partners[k]

                @pl.when(there & later)
                def _():
                    pl.semaphore_wait(own, 1)
                    second_z(k).start()

    pass_on(0)
    pass_on(1)
    square = product(load(h_a), load(h_a))
    f_b[...] = square
    store(h_b, square)
    store(h_inv2, eye + f_a[...] + f_b[...] + product(load(h_a), load(h_b)))

    for g in range(2, len(GROUPS)):
        pass_on(g)

    def third(g, core):
        z0, n = GROUPS[g]
        ref = cb.at[0, pl.ds(z0, n)] if core == 0 else cb.at[1, :, pl.ds(z0, n)]
        return remote(ref, ref, bs.at[g], br.at[g], sib)

    def share(g):
        z0, n = GROUPS[g]

        @pl.when(c == 0)
        def _():
            for o in (1, 7, 2, 6, 3, 5, 4):
                second_x_wait(g, o)
            third(g, 0).start()

        @pl.when(c == 1)
        def _():
            for k in range(z0, z0 + n):
                @pl.when(z != k)
                def _():
                    second_z_wait(k)
            third(g, 1).start()

    share(0)
    share(1)
    own_r.wait()
    for k in (0, 1, 4, 5, 6, 7):
        r_wait(k)
    first_rows = rb[0:4].reshape(B, 2 * 128)
    second_rows = rb[4:8].reshape(B, 2 * 128)
    u = product(load(h_inv1), split(first_rows))
    rest = second_rows - product(load(h_ll), split(u))
    share(2)
    y_two = split(product(load(h_inv2), split(rest)))
    h_y[0, B:], h_y[1, B:] = y_two
    h_y[0, :B], h_y[1, :B] = split(u - product(load(h_n), y_two))
    own_t.wait()

    def eliminate(g):
        z0, n = GROUPS[g]
        k0, kn = z0 * 128, n * 128

        @pl.when(c == 0)
        def _():
            third(g, 1).wait_recv()

        @pl.when(c == 1)
        def _():
            third(g, 0).wait_recv()

        blocks = []
        for a in range(z0, z0 + n):
            for b in range(N):
                blocks += [cb[0, a, b], cb[1, b, a]]
        left = jnp.concatenate(blocks, axis=0).T
        return product(split(left), (h_y[0, k0:k0 + kn], h_y[1, k0:k0 + kn]))

    trail[...] = trail[...] - eliminate(0)
    share(3)
    trail[...] = trail[...] - eliminate(1)
    share(4)
    trail[...] = trail[...] - eliminate(2)
    share(5)
    trail[...] = trail[...] - eliminate(3)
    trail[...] = trail[...] - eliminate(4)
    out_ref[...] = trail[...] - eliminate(5)

    for k in range(8):
        r_copy(k).wait_send()

    @pl.when(c == 0)
    def _():
        for k in range(N):
            @pl.when(z != k)
            def _():
                first_z(k).wait_send()

        for g in range(len(GROUPS)):
            for o in range(1, N):
                second_x(g, o).wait_send()
            third(g, 0).wait_send()

    @pl.when(c == 1)
    def _():
        for o in range(1, N):
            first_x(o).wait_send()
        for k in range(N):
            @pl.when(z != k)
            def _():
                second_z(k).wait_send()

        for g in range(len(GROUPS)):
            third(g, 1).wait_send()


def local_step(pivot, col_panel, row_panel, trailing):
    pair = pltpu.VMEM((2, B, B), BF16)
    return pl.pallas_call(
        kernel,
        out_shape=jax.ShapeDtypeStruct(trailing.shape, F32),
        in_specs=[pl.BlockSpec(memory_space=pl.ANY)] * 4,
        out_specs=pl.BlockSpec(memory_space=pltpu.VMEM),
        scratch_shapes=[
            pltpu.VMEM((2 * B, 2 * B), F32),
            pltpu.VMEM((N, 128, 256), F32),
            pltpu.VMEM((2, N, N, 8, B), F32),
            pltpu.VMEM((B, 256), F32),
            pltpu.VMEM((B, B), F32),
            pltpu.VMEM((B, B), F32),
            pair, pair, pair, pair, pair, pair,
            pltpu.VMEM((2, 2 * B, 256), BF16),
            pltpu.SemaphoreType.DMA((7,)),
            pltpu.SemaphoreType.DMA((N,)),
            pltpu.SemaphoreType.DMA((N,)),
            pltpu.SemaphoreType.DMA((len(GROUPS), N)),
            pltpu.SemaphoreType.DMA((len(GROUPS), N)),
            pltpu.SemaphoreType.DMA((N,)),
            pltpu.SemaphoreType.DMA((N,)),
            pltpu.SemaphoreType.DMA((len(GROUPS),)),
            pltpu.SemaphoreType.DMA((len(GROUPS),)),
            pltpu.SemaphoreType.DMA((8,)),
            pltpu.SemaphoreType.DMA((8,)),
            pltpu.SemaphoreType.REGULAR((N,)),
            pltpu.SemaphoreType.REGULAR((N,)),
            pltpu.SemaphoreType.REGULAR((4,)),
            pltpu.SemaphoreType.REGULAR((1,)),
        ],
        compiler_params=pltpu.CompilerParams(collective_id=0, has_side_effects=True, vmem_limit_bytes=56 << 20),
        name="eliminate",
    )(pivot, col_panel.T, row_panel, trailing)


def solution(mesh):
    return jax.shard_map(
        local_step,
        mesh=mesh,
        in_specs=(P(), P("row", "col"), P("row", "col"), P("row", "col")),
        out_specs=P("row", "col"),
        check_vma=False,
    )
```
